256 devices in a mesh: gx: 8 (over x, y_lo), gy: 8 (over z), gz: 4 (over y_hi, core).
Axes of the slice: x: 4, y: 4 (y_hi: 2, y_lo: 2; y = y_hi * 2 + y_lo), z: 8, core: 2. Of those that a mesh axis runs over, the one named last changes fastest.
Arguments:
- layer_input: bfloat16 [512, 8192], P(('gy', 'gz'), 'gx'), may hold values from -3 to 3
- out_grad: bfloat16 [512, 8192], P(('gy', 'gz'), 'gx'), may hold values from -1.5 to 1.5
- gate_pre: bfloat16 [512, 29568], P('gx', ('gy', 'gz')), may hold values from -8 to 8
- up_pre: bfloat16 [512, 29568], P('gx', ('gy', 'gz')), may hold values from -6 to 6
- gate_weight: bfloat16 [8192, 29568], P('gx', ('gy', 'gz')), may hold values from -0.0625 to 0.0625
- up_weight: bfloat16 [8192, 29568], P('gx', ('gy', 'gz')), may hold values from -0.0625 to 0.0625
- down_weight: bfloat16 [29568, 8192], P(('gy', 'gz'), 'gx'), may hold values from -0.03125 to 0.03125
Outputs:
- input_grad: bfloat16 [512, 8192], P(('gy', 'gz'), 'gx')
- gate_wgrad: bfloat16 [8192, 29568], P('gx', ('gy', 'gz'))
- up_wgrad: bfloat16 [8192, 29568], P('gx', ('gy', 'gz'))
- down_wgrad: bfloat16 [29568, 8192], P(('gy', 'gz'), 'gx')
The draws below stay inside these ranges and needn't reach their ends.
All inputs are finite; a program needn't handle non-finite values.
Results may differ from the reference program's by a relative error of at most 0.0054.
Values may be sent and summed in bfloat16 or wider, within the bound.
No kernel may reach another device: no remote copies, remote signals or barrier semaphores. Data moves between devices by JAX's collectives and lax.ppermute only.
A program may use at most 64 MiB of HBM per device.

```python
import jax
import jax.numpy as jnp

D = 8192
FF = 29568
TOKENS = 512


def block_scale(stream_key, shape, pieces, low, top_value):
    def one(dim, parts):
        heights = jax.random.uniform(jax.random.fold_in(jax.random.fold_in(stream_key, 6), dim), (parts,), jnp.float32, low / len(pieces), top_value / len(pieces))
        return jnp.repeat(jnp.exp(heights), shape[dim] // parts).reshape((-1,) + (1,) * (len(shape) - dim - 1))

    level = one(*pieces[0])
    for cut in pieces[1:]:
        level = level * one(*cut)
    return level


def noise(stream_key, extent, deviation, most, split=(), dtype=jnp.bfloat16):
    gain = block_scale(stream_key, extent, split, -0.22, 0.18) if split else 1.0
    array = jax.random.normal(stream_key, extent, jnp.float32) * deviation * gain
    return jnp.minimum(jnp.maximum(array, -most), most).astype(dtype)


def setup_inputs(seed: int = 0) -> dict:
    splits = jax.random.split(jax.random.key(seed), 8)
    layer_input = noise(splits[0], (TOKENS, D), 0.5, 3.0, ((0, 32), (1, 8)))
    out_grad = noise(splits[1], (TOKENS, D), 0.25, 1.5, ((0, 32), (1, 8)))
    gate_pre = noise(splits[2], (TOKENS, FF), 1.5, 8.0, ((0, 8), (1, 32)))
    up_pre = noise(splits[3], (TOKENS, FF), 1.0, 6.0, ((0, 8), (1, 32)))
    gate_weight = noise(splits[4], (D, FF), D ** -0.5, 0.0625, ((0, 8), (1, 32)))
    up_weight = noise(splits[5], (D, FF), D ** -0.5, 0.0625, ((0, 8), (1, 32)))
    down_weight = noise(splits[6], (FF, D), FF ** -0.5, 0.03125, ((0, 32), (1, 8)))
    return {"layer_input": layer_input, "out_grad": out_grad, "gate_pre": gate_pre, "up_pre": up_pre, "gate_weight": gate_weight, "up_weight": up_weight, "down_weight": down_weight}


def swiglu_back(hidden_grad, gate_pre, up_pre):
    gate = gate_pre.astype(jnp.float32)
    up_value = up_pre.astype(jnp.float32)
    sigmoid_gate = jax.nn.sigmoid(gate)
    activated = gate * sigmoid_gate
    hidden = (activated * up_value).astype(jnp.bfloat16)
    gate_grad = (hidden_grad * up_value * sigmoid_gate * (1.0 + gate * (1.0 - sigmoid_gate))).astype(jnp.bfloat16)
    up_grad = (hidden_grad * activated).astype(jnp.bfloat16)
    return gate_grad, up_grad, hidden


def reference(layer_input, out_grad, gate_pre, up_pre, gate_weight, up_weight, down_weight):
    hidden_grad = jnp.dot(out_grad, down_weight.T, preferred_element_type=jnp.float32)
    gate_grad, up_grad, hidden = swiglu_back(hidden_grad, gate_pre, up_pre)
    gate_wgrad = jnp.dot(layer_input.T, gate_grad, preferred_element_type=jnp.float32).astype(jnp.bfloat16)
    up_wgrad = jnp.dot(layer_input.T, up_grad, preferred_element_type=jnp.float32).astype(jnp.bfloat16)
    down_wgrad = jnp.dot(hidden.T, out_grad, preferred_element_type=jnp.float32).astype(jnp.bfloat16)
    input_grad = jnp.dot(gate_grad, gate_weight.T, preferred_element_type=jnp.float32)
    input_grad = input_grad + jnp.dot(up_grad, up_weight.T, preferred_element_type=jnp.float32)
    return input_grad.astype(jnp.bfloat16), gate_wgrad, up_wgrad, down_wgrad
```

```python
import jax
import jax.numpy as jnp
from jax import lax
from jax.experimental import pallas as pl
from jax.experimental.pallas import tpu as pltpu
from jax.sharding import PartitionSpec as P

F32 = jnp.float32
BF16 = jnp.bfloat16
BY_FEATURE = (((1,), (1,)), ((), ()))
BY_TOKEN = (((0,), (0,)), ((), ()))
ROWS = 16
NZ = 8

OWN = ((0, 0), (0, 1), (4, 0), (4, 1))
PREV = ((-1, 0), (-1, 1), (3, 0), (3, 1))
NEXT = ((1, 0), (1, 1), (5, 0), (5, 1))
PREV2 = ((-2, 0), (-2, 1))
NEXT2 = ((2, 0), (2, 1))
ORDER = OWN + PREV + NEXT + PREV2 + NEXT2


def gy_shift(step):
    return [(i, (i + step) % NZ) for i in range(NZ)]


def place_shift(step, flip):
    return [
        (z * 4 + g, ((z + step) % NZ) * 4 + (g ^ (2 * flip))) for z in range(NZ) for g in range(4)
    ]


OTHER_CORE = [(i, i ^ 1) for i in range(4)]
OTHER_Y = [(i, i ^ 2) for i in range(4)]


def place():
    gz = lax.axis_index("gz")
    return lax.axis_index("gy"), gz // 2, gz % 2


def row_of(here, there, core):
    z, y, _ = here
    step, flip = there
    block = lax.rem(z + step + NZ, NZ) * 4 + (y + flip - 2 * y * flip) * 2 + core
    return pl.multiple_of(block * ROWS, ROWS)


def gather_core(x):
    same_z = lax.ppermute(x, "gz", OTHER_Y)
    far = lax.ppermute(x, "gy", gy_shift(4))
    far_y = lax.ppermute(x, ("gy", "gz"), place_shift(4, 1))
    near = jnp.concatenate([x, same_z], axis=0)
    four = jnp.concatenate([near, far, far_y], axis=0)
    prev = lax.ppermute(four, "gy", gy_shift(1))
    following = lax.ppermute(four, "gy", gy_shift(-1))
    prev2 = lax.ppermute(near, "gy", gy_shift(2))
    following2 = lax.ppermute(near, "gy", gy_shift(-2))
    mine = jnp.concatenate([four, prev, following, prev2, following2], axis=0)
    other = lax.ppermute(mine, "gz", OTHER_CORE)
    return mine, other


def place_kernel(mine_ref, other_ref, out_ref):
    here = place()
    core = here[2]
    for k, there in enumerate(ORDER):
        rows = pl.ds(k * ROWS, ROWS)
        out_ref[pl.ds(row_of(here, there, core), ROWS), :] = mine_ref[rows, :]
        out_ref[pl.ds(row_of(here, there, 1 - core), ROWS), :] = other_ref[rows, :]


def place_rows(mine, other):
    rows, cols = mine.shape
    return pl.pallas_call(
        place_kernel,
        out_shape=jax.ShapeDtypeStruct((2 * rows, cols), mine.dtype),
        in_specs=[pl.BlockSpec(memory_space=pltpu.VMEM)] * 2,
        out_specs=pl.BlockSpec(memory_space=pltpu.VMEM),
        compiler_params=pltpu.CompilerParams(vmem_limit_bytes=16 * 2**20),
    )(mine, other)


def send_kernel(part_ref, out_ref):
    here = place()
    for k, there in enumerate(ORDER):
        out_ref[pl.ds(k * ROWS, ROWS), :] = part_ref[
            pl.ds(row_of(here, there, 1 - here[2]), ROWS), :
        ].astype(BF16)


def fold_kernel(part_ref, recv_ref, own_ref, prev_ref, next_ref, prev2_ref, next2_ref):
    here = place()
    k = 0
    for group, ref in (
        (OWN, own_ref),
        (PREV, prev_ref),
        (NEXT, next_ref),
        (PREV2, prev2_ref),
        (NEXT2, next2_ref),
    ):
        for j, there in enumerate(group):
            total = part_ref[pl.ds(row_of(here, there, here[2]), ROWS), :] + recv_ref[
                pl.ds(k * ROWS, ROWS), :
            ].astype(F32)
            ref[pl.ds(j * ROWS, ROWS), :] = total.astype(ref.dtype)
            k += 1


def scatter_rows(part):
    rows, cols = part.shape
    vmem = pl.BlockSpec(memory_space=pltpu.VMEM)
    params = pltpu.CompilerParams(vmem_limit_bytes=16 * 2**20)
    send = pl.pallas_call(
        send_kernel,
        out_shape=jax.ShapeDtypeStruct((rows // 2, cols), BF16),
        in_specs=[vmem],
        out_specs=vmem,
        compiler_params=params,
    )(part)
    recv = lax.ppermute(send, "gz", OTHER_CORE)
    own, prev, following, prev2, following2 = pl.pallas_call(
        fold_kernel,
        out_shape=(
            jax.ShapeDtypeStruct((64, cols), F32),
            jax.ShapeDtypeStruct((64, cols), BF16),
            jax.ShapeDtypeStruct((64, cols), BF16),
            jax.ShapeDtypeStruct((32, cols), BF16),
            jax.ShapeDtypeStruct((32, cols), BF16),
        ),
        in_specs=[vmem] * 2,
        out_specs=(vmem,) * 5,
        compiler_params=params,
    )(part, recv)
    from_next = lax.ppermute(prev, "gy", gy_shift(-1))
    from_prev = lax.ppermute(following, "gy", gy_shift(1))
    from_next2 = lax.ppermute(prev2, "gy", gy_shift(-2))
    from_prev2 = lax.ppermute(following2, "gy", gy_shift(2))
    total = own + from_next.astype(F32) + from_prev.astype(F32)
    near = total[:32] + from_next2.astype(F32) + from_prev2.astype(F32)
    far = total[32:].astype(BF16)
    got = (
        lax.ppermute(near[16:].astype(BF16), "gz", OTHER_Y),
        lax.ppermute(far[:16], "gy", gy_shift(4)),
        lax.ppermute(far[16:], ("gy", "gz"), place_shift(4, 1)),
    )
    return near[:16] + got[0].astype(F32) + got[1].astype(F32) + got[2].astype(F32)


def body(layer_input, out_grad, gate_pre, up_pre, gate_weight, up_weight, down_weight):
    pre = lax.all_gather(jnp.stack([gate_pre, up_pre]), "gx", axis=0)
    grad_cols = place_rows(*gather_core(out_grad))
    part = lax.dot_general(grad_cols, down_weight, BY_FEATURE, preferred_element_type=F32)
    tokens, units = part.shape
    block = tokens // 8
    parts = lax.all_to_all(part.astype(BF16).reshape(8, block, units), "gx", 0, 0)
    mine = jnp.sum(parts.astype(F32), axis=0).astype(BF16)
    hidden_grad = lax.all_to_all(jnp.broadcast_to(mine[None], (8, block, units)), "gx", 0, 0)
    hidden_grad = hidden_grad.reshape(tokens, units).astype(F32)
    gate = pre[:, 0].reshape(tokens, units).astype(F32)
    up_value = pre[:, 1].reshape(tokens, units).astype(F32)
    sigmoid_gate = jax.nn.sigmoid(gate)
    activated = gate * sigmoid_gate
    hidden = (activated * up_value).astype(BF16)
    gate_grad = (
        hidden_grad * up_value * sigmoid_gate * (1.0 + gate * (1.0 - sigmoid_gate))
    ).astype(BF16)
    up_grad = (hidden_grad * activated).astype(BF16)
    part_in = lax.dot_general(gate_grad, gate_weight, BY_FEATURE, preferred_element_type=F32)
    part_in = part_in + lax.dot_general(
        up_grad, up_weight, BY_FEATURE, preferred_element_type=F32
    )
    input_sum = scatter_rows(part_in)
    input_cols = place_rows(*gather_core(layer_input))
    gate_sum = lax.dot_general(input_cols, gate_grad, BY_TOKEN, preferred_element_type=F32)
    up_sum = lax.dot_general(input_cols, up_grad, BY_TOKEN, preferred_element_type=F32)
    down_sum = lax.dot_general(hidden, grad_cols, BY_TOKEN, preferred_element_type=F32)
    return (
        input_sum.astype(BF16),
        gate_sum.astype(BF16),
        up_sum.astype(BF16),
        down_sum.astype(BF16),
    )


def solution(mesh):
    tokens = P(("gy", "gz"), "gx")
    hidden = P("gx", ("gy", "gz"))
    return jax.shard_map(
        body,
        mesh=mesh,
        in_specs=(tokens, tokens, hidden, hidden, hidden, hidden, tokens),
        out_specs=(tokens, hidden, hidden, tokens),
        check_vma=False,
    )
```

```python
import jax
import jax.numpy as jnp
from jax import lax
from jax.experimental import pallas as pl
from jax.experimental.pallas import tpu as pltpu
from jax.sharding import PartitionSpec as P

F32 = jnp.float32
BF16 = jnp.bfloat16
BY_FEATURE = (((1,), (1,)), ((), ()))
BY_TOKEN = (((0,), (0,)), ((), ()))
ROWS = 16
NZ = 8

OWN = ((0, 0), (0, 1), (4, 0), (4, 1))
PREV = ((-1, 0), (-1, 1), (3, 0), (3, 1))
NEXT = ((1, 0), (1, 1), (5, 0), (5, 1))
PREV2 = ((-2, 0), (-2, 1))
NEXT2 = ((2, 0), (2, 1))
ORDER = OWN + PREV + NEXT + PREV2 + NEXT2


def gy_shift(step):
    return [(i, (i + step) % NZ) for i in range(NZ)]


def place_shift(step, flip):
    return [
        (z * 4 + g, ((z + step) % NZ) * 4 + (g ^ (2 * flip))) for z in range(NZ) for g in range(4)
    ]


OTHER_CORE = [(i, i ^ 1) for i in range(4)]
OTHER_Y = [(i, i ^ 2) for i in range(4)]
SAME_CORE = [[2 * k + core for k in range(16)] for core in range(2)]

ANY = pl.BlockSpec(memory_space=pl.ANY)
VMEM = pl.BlockSpec(memory_space=pltpu.VMEM)


def params(mib):
    return pltpu.CompilerParams(vmem_limit_bytes=mib * 2**20)


def row_of(there, second):
    z, y = lax.axis_index("gy"), lax.axis_index("gz") // 2
    step, flip = there
    block = lax.rem(z + step + NZ, NZ) * 4 + second * 2 + (y + flip - 2 * y * flip)
    return pl.multiple_of(block * ROWS, ROWS)


def far_places(x):
    return (
        lax.ppermute(x, ("gy", "gz"), place_shift(4, 1)),
        lax.ppermute(x, "gy", gy_shift(4)),
        lax.ppermute(x, "gz", OTHER_Y),
    )


def near_places(near, four):
    return (
        lax.ppermute(near, "gy", gy_shift(2)),
        lax.ppermute(near, "gy", gy_shift(-2)),
        lax.ppermute(four, "gy", gy_shift(1)),
        lax.ppermute(four, "gy", gy_shift(-1)),
    )


def swap_core(x):
    return lax.ppermute(x, "gz", OTHER_CORE)


def pair_kernel(x_ref, y_ref, out_ref, sems):
    copies = [
        pltpu.make_async_copy(ref, out_ref.at[pl.ds(k * ROWS, ROWS)], sems.at[k])
        for k, ref in enumerate((x_ref, y_ref))
    ]
    for copy in copies:
        copy.start()
    for copy in copies:
        copy.wait()


def pair(x, y):
    rows, cols = x.shape
    return pl.pallas_call(
        pair_kernel,
        out_shape=jax.ShapeDtypeStruct((2 * rows, cols), x.dtype),
        in_specs=[ANY] * 2,
        out_specs=VMEM,
        scratch_shapes=[pltpu.SemaphoreType.DMA((2,))],
        compiler_params=params(4),
    )(x, y)


def pack_kernel(x_ref, y_ref, far_ref, far_y_ref, _, *outs):
    for j in range(2):
        near_ref, four_ref = outs[2 * j : 2 * j + 2]
        for k, ref in enumerate((x_ref, y_ref, far_ref, far_y_ref)):
            rows = pl.ds(k * ROWS, ROWS)
            block = ref[j * ROWS : (j + 1) * ROWS, :]
            four_ref[rows, :] = block
            if k < 2:
                near_ref[rows, :] = block


def pack(x, far, earlier):
    far_y, far_z, same_z = far
    rows, cols = x.shape
    near = jax.ShapeDtypeStruct((rows, cols), x.dtype)
    four = jax.ShapeDtypeStruct((2 * rows, cols), x.dtype)
    return pl.pallas_call(
        pack_kernel,
        out_shape=(near, four, near, four),
        in_specs=[VMEM] * 4 + [ANY],
        out_specs=(VMEM,) * 4,
        compiler_params=params(4),
    )(x, same_z, far_z, far_y, earlier)


def merge_kernel(four_ref, prev_ref, next_ref, prev2_ref, next2_ref, *refs):
    out_ref = refs[-1]
    k = 0
    for ref in (four_ref, prev_ref, next_ref, prev2_ref, next2_ref):
        out_ref[pl.ds(k, ref.shape[0]), :] = ref[...]
        k += ref.shape[0]


def merge(four, got, earlier):
    prev2, next2, prev, following = got
    return pl.pallas_call(
        merge_kernel,
        out_shape=jax.ShapeDtypeStruct((16 * ROWS, four.shape[1]), four.dtype),
        in_specs=[VMEM] * 5 + [ANY] * len(earlier),
        out_specs=VMEM,
        compiler_params=params(4),
    )(four, prev, following, prev2, next2, *earlier)


def place_kernel(mine_ref, other_ref, out_ref):
    for k, there in enumerate(ORDER):
        rows = pl.ds(k * ROWS, ROWS)
        out_ref[pl.ds(row_of(there, 0), ROWS), :] = mine_ref[rows, :]
        out_ref[pl.ds(row_of(there, 1), ROWS), :] = other_ref[rows, :]


def place_rows(mine, other):
    rows, cols = mine.shape
    return pl.pallas_call(
        place_kernel,
        out_shape=jax.ShapeDtypeStruct((2 * rows, cols), mine.dtype),
        in_specs=[VMEM] * 2,
        out_specs=VMEM,
        compiler_params=params(8),
    )(mine, other)


def hidden_kernel(mine_ref, other_ref, weight_ref, _, cols_ref, out_ref):
    place_kernel(mine_ref, other_ref, cols_ref)
    part = lax.dot_general(
        cols_ref[...], weight_ref[...], BY_FEATURE, preferred_element_type=F32
    )
    out_ref[...] = part.astype(BF16).reshape(out_ref.shape)


def hidden_part(mine, other, weight, earlier):
    rows, cols = mine.shape
    return pl.pallas_call(
        hidden_kernel,
        out_shape=(
            jax.ShapeDtypeStruct((2 * rows, cols), BF16),
            jax.ShapeDtypeStruct((8, rows // 4, weight.shape[0]), BF16),
        ),
        in_specs=[VMEM, VMEM, VMEM, ANY],
        out_specs=(VMEM, VMEM),
        compiler_params=params(16),
    )(mine, other, weight, earlier)


def own_core_first(x):
    core = lax.axis_index("gz") % 2
    blocks = [x[k * ROWS : (k + 1) * ROWS, :] for k in range(4)]
    own = [jnp.where(core == 0, blocks[2 * y], blocks[2 * y + 1]) for y in range(2)]
    second = [jnp.where(core == 0, blocks[2 * y + 1], blocks[2 * y]) for y in range(2)]
    return jnp.concatenate(own + second, axis=0)


def local_hidden_kernel(gate_ref, up_ref, out_ref):
    gate = gate_ref[...].astype(F32)
    up_value = up_ref[...].astype(F32)
    out_ref[...] = own_core_first(gate * jax.nn.sigmoid(gate) * up_value).astype(BF16)


def local_hidden(gate, up):
    return pl.pallas_call(
        local_hidden_kernel,
        out_shape=jax.ShapeDtypeStruct(gate.shape, BF16),
        in_specs=[VMEM, VMEM],
        out_specs=VMEM,
        compiler_params=params(4),
    )(gate, up)


def sum_kernel(parts_ref, gate_ref, up_ref, _, out_ref):
    hidden_grad = parts_ref[0].astype(F32)
    for k in range(1, parts_ref.shape[0]):
        hidden_grad = hidden_grad + parts_ref[k].astype(F32)
    gate = own_core_first(gate_ref[...].astype(F32))
    up_value = own_core_first(up_ref[...].astype(F32))
    sigmoid_gate = jax.nn.sigmoid(gate)
    activated = gate * sigmoid_gate
    gate_grad = hidden_grad * up_value * sigmoid_gate * (1.0 + gate * (1.0 - sigmoid_gate))
    gate_grad = gate_grad.astype(BF16)
    up_grad = (hidden_grad * activated).astype(BF16)
    for k in range(out_ref.shape[0]):
        out_ref[k, 0] = gate_grad
        out_ref[k, 1] = up_grad


def grad_copies(parts, gate, up, earlier):
    blocks, rows, units = parts.shape
    return pl.pallas_call(
        sum_kernel,
        out_shape=jax.ShapeDtypeStruct((blocks, 2, rows, units), BF16),
        in_specs=[VMEM] * 3 + [ANY],
        out_specs=VMEM,
        compiler_params=params(8),
    )(parts, gate, up, earlier)


def stack_kernel(x_ref, y_ref, out_ref):
    rows = x_ref.shape[0]
    out_ref[:rows, :] = x_ref[...]
    out_ref[rows:, :] = y_ref[...]


def stack(x, y):
    rows, cols = x.shape
    return pl.pallas_call(
        stack_kernel,
        out_shape=jax.ShapeDtypeStruct((2 * rows, cols), x.dtype),
        in_specs=[VMEM] * 2,
        out_specs=VMEM,
        compiler_params=params(4),
    )(x, y)


def order_kernel(*refs):
    pieces, out_ref = refs[:4], refs[4]
    me = lax.axis_index("gx")
    rows = pieces[0].shape[0] // 2
    for step, ref in zip((0, 2, 6, 4), pieces):
        block = lax.rem(me + 8 - step, 8)
        for k in range(2):
            there = block + k * (1 - 2 * lax.rem(block, 2))
            out_ref[pl.ds(pl.multiple_of(there * rows, rows), rows), :] = ref[
                k * rows : (k + 1) * rows, :
            ]


def same_pair(x):
    return stack(x, lax.ppermute(x, "gx", [(i, i ^ 1) for i in range(8)]))


def along_x(pair):
    return [pair] + [
        lax.ppermute(pair, "gx", [(i, (i + step) % 8) for i in range(8)]) for step in (2, 6, 4)
    ]


def in_order(pieces):
    rows, units = pieces[0].shape
    return pl.pallas_call(
        order_kernel,
        out_shape=jax.ShapeDtypeStruct((4 * rows, units), pieces[0].dtype),
        in_specs=[VMEM] * 4,
        out_specs=VMEM,
        compiler_params=params(8),
    )(*pieces)


def last_sum_kernel(parts_ref, out_ref):
    total = parts_ref[0].astype(F32)
    for k in range(1, parts_ref.shape[0]):
        total = total + parts_ref[k].astype(F32)
    out_ref[...] = total.astype(BF16)


def last_sum(parts):
    return pl.pallas_call(
        last_sum_kernel,
        out_shape=jax.ShapeDtypeStruct(parts.shape[1:], BF16),
        in_specs=[VMEM],
        out_specs=VMEM,
        compiler_params=params(4),
    )(parts)


def input_kernel(grads_ref, gw_ref, uw_ref, send_ref, keep_ref):
    blocks, _, rows, units = grads_ref.shape
    half = rows // 2
    for k, ref in enumerate((send_ref, keep_ref)):
        part = pl.ds((1 - k) * half, half)
        gate_grad = grads_ref[:, 0, part, :].reshape(blocks * half, units)
        up_grad = grads_ref[:, 1, part, :].reshape(blocks * half, units)
        ref[...] = jnp.dot(gate_grad, gw_ref[...], preferred_element_type=F32) + jnp.dot(
            up_grad, uw_ref[...], preferred_element_type=F32
        )


def input_parts(grads, gate_weight, up_weight):
    blocks, _, rows, _ = grads.shape
    half = jax.ShapeDtypeStruct((blocks * rows // 2, gate_weight.shape[1]), F32)
    return pl.pallas_call(
        input_kernel,
        out_shape=(half, half),
        in_specs=[VMEM] * 3,
        out_specs=(VMEM, VMEM),
        compiler_params=params(16),
    )(grads, gate_weight, up_weight)


def body(layer_input, out_grad, gate_pre, up_pre, gate_weight, up_weight, down_weight):
    both = pair(out_grad, layer_input)
    far = far_places(both)
    hidden_pair = same_pair(local_hidden(gate_pre, up_pre))
    near, four, near_in, four_in = pack(both, far, hidden_pair)
    pieces = along_x(hidden_pair)
    mine = merge(four, near_places(near, four), pieces[1:])
    hidden = in_order(pieces)
    grad_cols, part = hidden_part(mine, swap_core(mine), down_weight, hidden)
    parts = lax.all_to_all(part, "gx", 0, 0)
    mine_in = merge(four_in, near_places(near_in, four_in), [])
    grads = lax.all_to_all(grad_copies(parts, gate_pre, up_pre, mine_in), "gx", 0, 0)
    send, keep = input_parts(grads, gate_weight.T, up_weight.T)
    total = (keep + swap_core(send)).astype(BF16).reshape(16, ROWS, -1)
    totals = lax.all_to_all(total, ("gy", "gz"), 0, 0, axis_index_groups=SAME_CORE)
    input_sum = last_sum(totals)
    gate_grad, up_grad = grads[:, 0].reshape(512, -1), grads[:, 1].reshape(512, -1)
    input_cols = place_rows(mine_in, swap_core(mine_in))
    gate_sum = lax.dot_general(input_cols, gate_grad, BY_TOKEN, preferred_element_type=F32)
    up_sum = lax.dot_general(input_cols, up_grad, BY_TOKEN, preferred_element_type=F32)
    down_sum = lax.dot_general(hidden, grad_cols, BY_TOKEN, preferred_element_type=F32)
    return (
        input_sum,
        gate_sum.astype(BF16),
        up_sum.astype(BF16),
        down_sum.astype(BF16),
    )


def solution(mesh):
    tokens = P(("gy", "gz"), "gx")
    hidden = P("gx", ("gy", "gz"))
    return jax.shard_map(
        body,
        mesh=mesh,
        in_specs=(tokens, tokens, hidden, hidden, hidden, hidden, tokens),
        out_specs=(tokens, hidden, hidden, tokens),
        check_vma=False,
    )
```

```python
import functools

import jax
import jax.numpy as jnp
from jax import lax
from jax.experimental import pallas as pl
from jax.experimental.pallas import tpu as pltpu
from jax.sharding import PartitionSpec as P

F32 = jnp.float32
BF16 = jnp.bfloat16
BY_FEATURE = (((1,), (1,)), ((), ()))
BY_TOKEN = (((0,), (0,)), ((), ()))
ROWS = 16
NZ = 8

OWN = ((0, 0), (0, 1), (4, 0), (4, 1))
PREV = ((-1, 0), (-1, 1), (3, 0), (3, 1))
NEXT = ((1, 0), (1, 1), (5, 0), (5, 1))
PREV2 = ((-2, 0), (-2, 1))
NEXT2 = ((2, 0), (2, 1))
ORDER = OWN + PREV + NEXT + PREV2 + NEXT2


def gy_shift(step):
    return [(i, (i + step) % NZ) for i in range(NZ)]


def place_shift(step, flip):
    return [
        (z * 4 + g, ((z + step) % NZ) * 4 + (g ^ (2 * flip))) for z in range(NZ) for g in range(4)
    ]


OTHER_CORE = [(i, i ^ 1) for i in range(4)]
OTHER_Y = [(i, i ^ 2) for i in range(4)]
FAR_PLACES = [
    [(z + 4 * a) * 4 + 2 * y + core for a in range(2) for y in range(2)]
    for z in range(4)
    for core in range(2)
]
SAME_CORE = [[2 * k + core for k in range(16)] for core in range(2)]

ANY = pl.BlockSpec(memory_space=pl.ANY)
VMEM = pl.BlockSpec(memory_space=pltpu.VMEM)


def params(mib):
    return pltpu.CompilerParams(vmem_limit_bytes=mib * 2**20)


def row_of(there, second):
    z, y = lax.axis_index("gy"), lax.axis_index("gz") // 2
    step, flip = there
    block = second * 2 * NZ + lax.rem(z + step + NZ, NZ) * 2 + (y + flip - 2 * y * flip)
    return pl.multiple_of(block * ROWS, ROWS)


def near_places(near, four):
    return (
        lax.ppermute(near, "gy", gy_shift(2)),
        lax.ppermute(near, "gy", gy_shift(-2)),
        lax.ppermute(four, "gy", gy_shift(1)),
        lax.ppermute(four, "gy", gy_shift(-1)),
    )


def swap_core(x):
    return lax.ppermute(x, "gz", OTHER_CORE)


def pair_kernel(x_in, y_in, _, out_ref, held, sems):
    copies = [
        pltpu.make_async_copy(ref, held.at[pl.ds(k * ROWS, ROWS)], sems.at[k])
        for k, ref in enumerate((x_in, y_in))
    ]
    for copy in copies:
        copy.start()
    for copy in copies:
        copy.wait()
    for k in range(out_ref.shape[0]):
        out_ref[k] = held[...]


def pair_copies(x, y, earlier):
    rows, cols = x.shape
    return pl.pallas_call(
        pair_kernel,
        out_shape=jax.ShapeDtypeStruct((4, 2 * rows, cols), x.dtype),
        in_specs=[ANY] * 3,
        out_specs=VMEM,
        scratch_shapes=[pltpu.VMEM((2 * rows, cols), BF16), pltpu.SemaphoreType.DMA((2,))],
        compiler_params=params(58),
    )(x, y, earlier)


def far_places(x, y, earlier):
    return lax.all_to_all(
        pair_copies(x, y, earlier), ("gy", "gz"), 0, 0, axis_index_groups=FAR_PLACES
    )


def pack_kernel(far_ref, _, *outs):
    a, y = lax.axis_index("gy") // 4, lax.axis_index("gz") // 2
    for k, (far, flip) in enumerate(((0, 0), (0, 1), (1, 0), (1, 1))):
        there = (a + far - 2 * a * far) * 2 + (y + flip - 2 * y * flip)
        rows = pl.ds(k * ROWS, ROWS)
        for j in range(2):
            near_ref, four_ref = outs[2 * j : 2 * j + 2]
            block = far_ref[there, j * ROWS : (j + 1) * ROWS, :]
            four_ref[rows, :] = block
            if k < 2:
                near_ref[rows, :] = block


def pack(far, earlier):
    _, rows, cols = far.shape
    near = jax.ShapeDtypeStruct((rows, cols), far.dtype)
    four = jax.ShapeDtypeStruct((2 * rows, cols), far.dtype)
    return pl.pallas_call(
        pack_kernel,
        out_shape=(near, four, near, four),
        in_specs=[VMEM, ANY],
        out_specs=(VMEM,) * 4,
        compiler_params=params(4),
    )(far, earlier)


def merge_kernel(four_ref, prev_ref, next_ref, prev2_ref, next2_ref, *refs):
    out_ref = refs[-1]
    k = 0
    for ref in (four_ref, prev_ref, next_ref, prev2_ref, next2_ref):
        out_ref[pl.ds(k, ref.shape[0]), :] = ref[...]
        k += ref.shape[0]


def merge(four, got, earlier):
    prev2, next2, prev, following = got
    return pl.pallas_call(
        merge_kernel,
        out_shape=jax.ShapeDtypeStruct((16 * ROWS, four.shape[1]), four.dtype),
        in_specs=[VMEM] * 5 + [ANY] * len(earlier),
        out_specs=VMEM,
        compiler_params=params(4),
    )(four, prev, following, prev2, next2, *earlier)


def place_kernel(mine_ref, other_ref, out_ref):
    for k, there in enumerate(ORDER):
        rows = pl.ds(k * ROWS, ROWS)
        out_ref[pl.ds(row_of(there, 0), ROWS), :] = mine_ref[rows, :]
        out_ref[pl.ds(row_of(there, 1), ROWS), :] = other_ref[rows, :]


def place_rows(mine, other):
    rows, cols = mine.shape
    return pl.pallas_call(
        place_kernel,
        out_shape=jax.ShapeDtypeStruct((2 * rows, cols), mine.dtype),
        in_specs=[VMEM] * 2,
        out_specs=VMEM,
        compiler_params=params(8),
    )(mine, other)


def hidden_kernel(mine_ref, other_ref, weight_ref, *refs):
    cols_ref, out_ref = refs[-2:]
    place_kernel(mine_ref, other_ref, cols_ref)
    blocks, rows, units = out_ref.shape
    half = blocks * rows // 2
    for k in range(2):
        part = lax.dot_general(
            cols_ref[pl.ds(k * half, half), :],
            weight_ref[...],
            BY_FEATURE,
            preferred_element_type=F32,
        )
        out_ref[:, pl.ds(k * rows // 2, rows // 2), :] = part.astype(BF16).reshape(
            blocks, rows // 2, units
        )


def hidden_part(mine, other, weight, earlier):
    rows, cols = mine.shape
    return pl.pallas_call(
        hidden_kernel,
        out_shape=(
            jax.ShapeDtypeStruct((2 * rows, cols), BF16),
            jax.ShapeDtypeStruct((8, rows // 4, weight.shape[0]), BF16),
        ),
        in_specs=[VMEM] * 3 + [ANY] * len(earlier),
        out_specs=(VMEM, VMEM),
        compiler_params=params(16),
    )(mine, other, weight, *earlier)


def pre_kernel(gate_in, up_in, out_ref, held, sems):
    core = lax.axis_index("gz") % 2
    loads = [
        pltpu.make_async_copy(ref, held.at[k], sems.at[k]) for k, ref in enumerate((gate_in, up_in))
    ]
    for load in loads:
        load.start()
    for k, load in enumerate(loads):
        load.wait()
        blocks = [held[k, j * ROWS : (j + 1) * ROWS, :] for j in range(4)]
        for y in range(2):
            for second in range(2):
                out_ref[pl.ds((4 * k + 2 * second + y) * ROWS, ROWS), :] = jnp.where(
                    core == 0, blocks[2 * y + second], blocks[2 * y + 1 - second]
                )


def pack_pre(gate, up):
    rows, units = gate.shape
    return pl.pallas_call(
        pre_kernel,
        out_shape=jax.ShapeDtypeStruct((2 * rows, units), gate.dtype),
        in_specs=[ANY] * 2,
        out_specs=VMEM,
        scratch_shapes=[pltpu.VMEM((2, rows, units), BF16), pltpu.SemaphoreType.DMA((2,))],
        compiler_params=params(58),
    )(gate, up)


def sum_kernel(parts_ref, *refs):
    out_ref = refs[-1]
    total = parts_ref[0].astype(F32)
    for k in range(1, parts_ref.shape[0]):
        total = total + parts_ref[k].astype(F32)
    total = total.astype(BF16)
    for k in range(out_ref.shape[0]):
        out_ref[k] = total


def sum_copies(parts, earlier):
    return pl.pallas_call(
        sum_kernel,
        out_shape=jax.ShapeDtypeStruct(parts.shape, BF16),
        in_specs=[VMEM] + [ANY] * len(earlier),
        out_specs=VMEM,
        compiler_params=params(8),
    )(parts, *earlier)


def stack_kernel(x_ref, y_ref, out_ref):
    rows = x_ref.shape[0]
    out_ref[:rows, :] = x_ref[...]
    out_ref[rows:, :] = y_ref[...]


def stack(x, y):
    rows, cols = x.shape
    return pl.pallas_call(
        stack_kernel,
        out_shape=jax.ShapeDtypeStruct((2 * rows, cols), x.dtype),
        in_specs=[VMEM] * 2,
        out_specs=VMEM,
        compiler_params=params(4),
    )(x, y)


STEPS = (0, 2, 6, 4)


def blocks_of(pieces):
    me = lax.axis_index("gx")
    rows = pieces[0].shape[0] // 4
    for step, ref in zip(STEPS, pieces):
        block = lax.rem(me + 8 - step, 8)
        for k in range(2):
            yield block + k * (1 - 2 * lax.rem(block, 2)), ref, 2 * k * rows, rows


def hidden_rows_kernel(*refs):
    pieces, out_ref = refs[:4], refs[-1]
    for block, ref, first, rows in blocks_of(pieces):
        gate = ref[first : first + rows, :].astype(F32)
        up_value = ref[first + rows : first + 2 * rows, :].astype(F32)
        hidden = (gate * jax.nn.sigmoid(gate) * up_value).astype(BF16)
        for k in range(2):
            out_ref[k, block] = hidden[k * rows // 2 : (k + 1) * rows // 2, :]


def hidden_rows(pieces):
    rows, units = pieces[0].shape
    return pl.pallas_call(
        hidden_rows_kernel,
        out_shape=jax.ShapeDtypeStruct((2, 8, rows // 8, units), BF16),
        in_specs=[VMEM] * 4,
        out_specs=VMEM,
        compiler_params=params(12),
    )(*pieces)


def same_pair(x):
    return stack(x, lax.ppermute(x, "gx", [(i, i ^ 1) for i in range(8)]))


def along_x(pair):
    return [pair] + [
        lax.ppermute(pair, "gx", [(i, (i + step) % 8) for i in range(8)]) for step in (2, 6, 4)
    ]


def last_sum_kernel(parts_ref, out_ref):
    total = parts_ref[0].astype(F32)
    for k in range(1, parts_ref.shape[0]):
        total = total + parts_ref[k].astype(F32)
    out_ref[...] = total.astype(BF16)


def last_sum(parts):
    return pl.pallas_call(
        last_sum_kernel,
        out_shape=jax.ShapeDtypeStruct(parts.shape[1:], BF16),
        in_specs=[VMEM],
        out_specs=VMEM,
        compiler_params=params(4),
    )(parts)


def input_kernel(k, *refs):
    pieces, (hid_ref, gw_ref, uw_ref), refs = refs[:4], refs[4:7], refs[7:]
    part_ref, gg_ref, ug_ref = refs[-3:]
    half = hid_ref.shape[1] // 2
    gate_grads, up_grads, places = [], [], []
    for block, piece, first, rows in blocks_of(pieces):
        hidden_grad = hid_ref[block, k * half : (k + 1) * half, :].astype(F32)
        gate = piece[first + k * half : first + (k + 1) * half, :].astype(F32)
        first = first + rows
        up_value = piece[first + k * half : first + (k + 1) * half, :].astype(F32)
        sigmoid_gate = jax.nn.sigmoid(gate)
        gate_grad = hidden_grad * up_value * sigmoid_gate * (1.0 + gate * (1.0 - sigmoid_gate))
        gate_grads.append(gate_grad.astype(BF16))
        up_grads.append((hidden_grad * (gate * sigmoid_gate)).astype(BF16))
        places.append(block)
        gg_ref[k, block] = gate_grads[-1]
        ug_ref[k, block] = up_grads[-1]
    if len(refs) > 3:
        gg_ref[1 - k] = refs[0][1 - k]
        ug_ref[1 - k] = refs[1][1 - k]
    part = jnp.dot(
        jnp.concatenate(gate_grads, axis=0), gw_ref[...], preferred_element_type=F32
    ) + jnp.dot(jnp.concatenate(up_grads, axis=0), uw_ref[...], preferred_element_type=F32)
    for j, block in enumerate(places):
        part_ref[block] = part[j * half : (j + 1) * half, :]


def input_part(k, hidden_grad, pieces, gate_weight, up_weight, grads):
    blocks, rows, units = hidden_grad.shape
    half = jax.ShapeDtypeStruct((blocks, rows // 2, gate_weight.shape[1]), F32)
    grad = jax.ShapeDtypeStruct((2, blocks, rows // 2, units), BF16)
    return pl.pallas_call(
        functools.partial(input_kernel, k),
        out_shape=(half, grad, grad),
        in_specs=[VMEM] * (7 + len(grads)),
        out_specs=(VMEM,) * 3,
        compiler_params=params(12),
    )(*pieces, hidden_grad, gate_weight, up_weight, *grads)


def body(layer_input, out_grad, gate_pre, up_pre, gate_weight, up_weight, down_weight):
    pre = pack_pre(gate_pre, up_pre)
    far = far_places(out_grad, layer_input, pre)
    pre_pair = same_pair(pre)
    near, four, near_in, four_in = pack(far, pre_pair)
    pieces = along_x(pre_pair)
    mine = merge(four, near_places(near, four), pieces[1:])
    grad_cols, part = hidden_part(mine, swap_core(mine), down_weight, [])
    parts = lax.all_to_all(part, "gx", 0, 0)
    mine_in = merge(four_in, near_places(near_in, four_in), [])
    hidden_grad = lax.all_to_all(sum_copies(parts, [mine_in]), "gx", 0, 0)
    weights = (gate_weight.T, up_weight.T)
    send, gate_grad, up_grad = input_part(1, hidden_grad, pieces, *weights, [])
    keep, gate_grad, up_grad = input_part(
        0, hidden_grad, pieces, *weights, [gate_grad, up_grad]
    )
    total = (keep + swap_core(send)).astype(BF16).reshape(16, ROWS, -1)
    totals = lax.all_to_all(total, ("gy", "gz"), 0, 0, axis_index_groups=SAME_CORE)
    input_sum = last_sum(totals)
    hidden = hidden_rows(pieces)
    gate_grad, up_grad, hidden = (v.reshape(512, -1) for v in (gate_grad, up_grad, hidden))
    input_cols = place_rows(mine_in, swap_core(mine_in))
    gate_sum = lax.dot_general(input_cols, gate_grad, BY_TOKEN, preferred_element_type=F32)
    up_sum = lax.dot_general(input_cols, up_grad, BY_TOKEN, preferred_element_type=F32)
    down_sum = lax.dot_general(hidden, grad_cols, BY_TOKEN, preferred_element_type=F32)
    return (
        input_sum,
        gate_sum.astype(BF16),
        up_sum.astype(BF16),
        down_sum.astype(BF16),
    )


def solution(mesh):
    tokens = P(("gy", "gz"), "gx")
    hidden = P("gx", ("gy", "gz"))
    return jax.shard_map(
        body,
        mesh=mesh,
        in_specs=(tokens, tokens, hidden, hidden, hidden, hidden, tokens),
        out_specs=(tokens, hidden, hidden, tokens),
        check_vma=False,
    )
```

```python
import functools

import jax
import jax.numpy as jnp
from jax import lax
from jax.experimental import pallas as pl
from jax.experimental.pallas import tpu as pltpu
from jax.sharding import PartitionSpec as P

F32 = jnp.float32
BF16 = jnp.bfloat16
BY_FEATURE = (((1,), (1,)), ((), ()))
BY_TOKEN = (((0,), (0,)), ((), ()))
ROWS = 16
NZ = 8

OWN = ((0, 0), (0, 1), (4, 0), (4, 1))
PREV = ((-1, 0), (-1, 1), (3, 0), (3, 1))
NEXT = ((1, 0), (1, 1), (5, 0), (5, 1))
PREV2 = ((-2, 0), (-2, 1))
NEXT2 = ((2, 0), (2, 1))
ORDER = OWN + PREV + NEXT + PREV2 + NEXT2


def gy_shift(step):
    return [(i, (i + step) % NZ) for i in range(NZ)]


OTHER_CORE = [(i, i ^ 1) for i in range(4)]
FAR_PLACES = [
    [(z + 4 * a) * 4 + 2 * y + core for a in range(2) for y in range(2)]
    for z in range(4)
    for core in range(2)
]
SAME_CORE = [[2 * k + core for k in range(16)] for core in range(2)]

ANY = pl.BlockSpec(memory_space=pl.ANY)
VMEM = pl.BlockSpec(memory_space=pltpu.VMEM)


def params(mib):
    return pltpu.CompilerParams(vmem_limit_bytes=mib * 2**20)


def row_of(there, second):
    z, y = lax.axis_index("gy"), lax.axis_index("gz") // 2
    step, flip = there
    block = second * 2 * NZ + lax.rem(z + step + NZ, NZ) * 2 + (y + flip - 2 * y * flip)
    return pl.multiple_of(block * ROWS, ROWS)


def near_places(near, four):
    return (
        lax.ppermute(near, "gy", gy_shift(2)),
        lax.ppermute(near, "gy", gy_shift(-2)),
        lax.ppermute(four, "gy", gy_shift(1)),
        lax.ppermute(four, "gy", gy_shift(-1)),
    )


def swap_core(x):
    return lax.ppermute(x, "gz", OTHER_CORE)


def front_kernel(*refs):
    ins, (far_ref, pre_ref, tokens, held, sems) = refs[:4], refs[4:]
    parts = (tokens.at[pl.ds(0, ROWS)], tokens.at[pl.ds(ROWS, ROWS)], held.at[0], held.at[1])
    loads = [
        pltpu.make_async_copy(src, dst, sems.at[k]) for k, (src, dst) in enumerate(zip(ins, parts))
    ]
    for load in loads:
        load.start()
    for load in loads:
        load.wait()
    core = lax.axis_index("gz") % 2
    for k in range(2):
        blocks = [held[k, j * ROWS : (j + 1) * ROWS, :] for j in range(4)]
        for y in range(2):
            for second in range(2):
                pre_ref[pl.ds((4 * k + 2 * second + y) * ROWS, ROWS), :] = jnp.where(
                    core == 0, blocks[2 * y + second], blocks[2 * y + 1 - second]
                )
    for k in range(far_ref.shape[0]):
        far_ref[k] = tokens[...]


def front(x, y, gate, up):
    rows, units = gate.shape
    return pl.pallas_call(
        front_kernel,
        out_shape=(
            jax.ShapeDtypeStruct((4, 2 * ROWS, x.shape[1]), BF16),
            jax.ShapeDtypeStruct((2 * rows, units), BF16),
        ),
        in_specs=[ANY] * 4,
        out_specs=(VMEM, VMEM),
        scratch_shapes=[
            pltpu.VMEM((2 * ROWS, x.shape[1]), BF16),
            pltpu.VMEM((2, rows, units), BF16),
            pltpu.SemaphoreType.DMA((4,)),
        ],
        compiler_params=params(58),
    )(x, y, gate, up)


def pack_kernel(far_ref, _, *outs):
    a, y = lax.axis_index("gy") // 4, lax.axis_index("gz") // 2
    for k, (far, flip) in enumerate(((0, 0), (0, 1), (1, 0), (1, 1))):
        there = (a + far - 2 * a * far) * 2 + (y + flip - 2 * y * flip)
        rows = pl.ds(k * ROWS, ROWS)
        for j in range(2):
            near_ref, four_ref = outs[2 * j : 2 * j + 2]
            block = far_ref[there, j * ROWS : (j + 1) * ROWS, :]
            four_ref[rows, :] = block
            if k < 2:
                near_ref[rows, :] = block


def pack(far, earlier):
    _, rows, cols = far.shape
    near = jax.ShapeDtypeStruct((rows, cols), far.dtype)
    four = jax.ShapeDtypeStruct((2 * rows, cols), far.dtype)
    return pl.pallas_call(
        pack_kernel,
        out_shape=(near, four, near, four),
        in_specs=[VMEM, ANY],
        out_specs=(VMEM,) * 4,
        compiler_params=params(4),
    )(far, earlier)


def merge_kernel(four_ref, prev_ref, next_ref, prev2_ref, next2_ref, *refs):
    out_ref = refs[-1]
    k = 0
    for ref in (four_ref, prev_ref, next_ref, prev2_ref, next2_ref):
        out_ref[pl.ds(k, ref.shape[0]), :] = ref[...]
        k += ref.shape[0]


def merge(four, got, earlier):
    prev2, next2, prev, following = got
    return pl.pallas_call(
        merge_kernel,
        out_shape=jax.ShapeDtypeStruct((16 * ROWS, four.shape[1]), four.dtype),
        in_specs=[VMEM] * 5 + [ANY] * len(earlier),
        out_specs=VMEM,
        compiler_params=params(4),
    )(four, prev, following, prev2, next2, *earlier)


def place_kernel(mine_ref, other_ref, out_ref):
    for k, there in enumerate(ORDER):
        rows = pl.ds(k * ROWS, ROWS)
        out_ref[pl.ds(row_of(there, 0), ROWS), :] = mine_ref[rows, :]
        out_ref[pl.ds(row_of(there, 1), ROWS), :] = other_ref[rows, :]


def place_rows(mine, other):
    rows, cols = mine.shape
    return pl.pallas_call(
        place_kernel,
        out_shape=jax.ShapeDtypeStruct((2 * rows, cols), mine.dtype),
        in_specs=[VMEM] * 2,
        out_specs=VMEM,
        compiler_params=params(8),
    )(mine, other)


def hidden_kernel(mine_ref, other_ref, weight_ref, *refs):
    cols_ref, out_ref = refs[-2:]
    place_kernel(mine_ref, other_ref, cols_ref)
    blocks, rows, units = out_ref.shape
    half = blocks * rows // 2
    for k in range(2):
        part = lax.dot_general(
            cols_ref[pl.ds(k * half, half), :],
            weight_ref[...],
            BY_FEATURE,
            preferred_element_type=F32,
        )
        out_ref[:, pl.ds(k * rows // 2, rows // 2), :] = part.astype(BF16).reshape(
            blocks, rows // 2, units
        )


def hidden_part(mine, other, weight, earlier):
    rows, cols = mine.shape
    return pl.pallas_call(
        hidden_kernel,
        out_shape=(
            jax.ShapeDtypeStruct((2 * rows, cols), BF16),
            jax.ShapeDtypeStruct((8, rows // 4, weight.shape[0]), BF16),
        ),
        in_specs=[VMEM] * 3 + [ANY] * len(earlier),
        out_specs=(VMEM, VMEM),
        compiler_params=params(16),
    )(mine, other, weight, *earlier)


def sum_kernel(parts_ref, *refs):
    out_ref = refs[-1]
    total = parts_ref[0].astype(F32)
    for k in range(1, parts_ref.shape[0]):
        total = total + parts_ref[k].astype(F32)
    total = total.astype(BF16)
    for k in range(out_ref.shape[0]):
        out_ref[k] = total


def sum_copies(parts, earlier):
    return pl.pallas_call(
        sum_kernel,
        out_shape=jax.ShapeDtypeStruct(parts.shape, BF16),
        in_specs=[VMEM] + [ANY] * len(earlier),
        out_specs=VMEM,
        compiler_params=params(8),
    )(parts, *earlier)


def stack_kernel(x_ref, y_ref, out_ref):
    rows = x_ref.shape[0]
    out_ref[:rows, :] = x_ref[...]
    out_ref[rows:, :] = y_ref[...]


def stack(x, y):
    rows, cols = x.shape
    return pl.pallas_call(
        stack_kernel,
        out_shape=jax.ShapeDtypeStruct((2 * rows, cols), x.dtype),
        in_specs=[VMEM] * 2,
        out_specs=VMEM,
        compiler_params=params(4),
    )(x, y)


STEPS = (0, 2, 6, 4)


def blocks_of(pieces):
    me = lax.axis_index("gx")
    rows = pieces[0].shape[0] // 4
    for step, ref in zip(STEPS, pieces):
        block = lax.rem(me + 8 - step, 8)
        for k in range(2):
            yield block + k * (1 - 2 * lax.rem(block, 2)), ref, 2 * k * rows, rows


def hidden_rows_kernel(*refs):
    pieces, out_ref = refs[:4], refs[-1]
    for block, ref, first, rows in blocks_of(pieces):
        gate = ref[first : first + rows, :].astype(F32)
        up_value = ref[first + rows : first + 2 * rows, :].astype(F32)
        hidden = (gate * jax.nn.sigmoid(gate) * up_value).astype(BF16)
        for k in range(2):
            out_ref[k, block] = hidden[k * rows // 2 : (k + 1) * rows // 2, :]


def hidden_rows(pieces):
    rows, units = pieces[0].shape
    return pl.pallas_call(
        hidden_rows_kernel,
        out_shape=jax.ShapeDtypeStruct((2, 8, rows // 8, units), BF16),
        in_specs=[VMEM] * 4,
        out_specs=VMEM,
        compiler_params=params(12),
    )(*pieces)


def same_pair(x):
    return stack(x, lax.ppermute(x, "gx", [(i, i ^ 1) for i in range(8)]))


def along_x(pair):
    return [pair] + [
        lax.ppermute(pair, "gx", [(i, (i + step) % 8) for i in range(8)]) for step in (2, 6, 4)
    ]


def last_sum_kernel(parts_ref, out_ref):
    total = parts_ref[0].astype(F32)
    for k in range(1, parts_ref.shape[0]):
        total = total + parts_ref[k].astype(F32)
    out_ref[...] = total.astype(BF16)


def last_sum(parts):
    return pl.pallas_call(
        last_sum_kernel,
        out_shape=jax.ShapeDtypeStruct(parts.shape[1:], BF16),
        in_specs=[VMEM],
        out_specs=VMEM,
        compiler_params=params(4),
    )(parts)


def input_kernel(k, *refs):
    pieces, (hid_ref, gw_ref, uw_ref), refs = refs[:4], refs[4:7], refs[7:]
    part_ref, gg_ref, ug_ref = refs[-3:]
    half = hid_ref.shape[1] // 2
    gate_grads, up_grads, places = [], [], []
    for block, piece, first, rows in blocks_of(pieces):
        hidden_grad = hid_ref[block, k * half : (k + 1) * half, :].astype(F32)
        gate = piece[first + k * half : first + (k + 1) * half, :].astype(F32)
        first = first + rows
        up_value = piece[first + k * half : first + (k + 1) * half, :].astype(F32)
        sigmoid_gate = jax.nn.sigmoid(gate)
        gate_grad = hidden_grad * up_value * sigmoid_gate * (1.0 + gate * (1.0 - sigmoid_gate))
        gate_grads.append(gate_grad.astype(BF16))
        up_grads.append((hidden_grad * (gate * sigmoid_gate)).astype(BF16))
        places.append(block)
        gg_ref[k, block] = gate_grads[-1]
        ug_ref[k, block] = up_grads[-1]
    if len(refs) > 3:
        gg_ref[1 - k] = refs[0][1 - k]
        ug_ref[1 - k] = refs[1][1 - k]
    part = jnp.dot(
        jnp.concatenate(gate_grads, axis=0), gw_ref[...], preferred_element_type=F32
    ) + jnp.dot(jnp.concatenate(up_grads, axis=0), uw_ref[...], preferred_element_type=F32)
    for j, block in enumerate(places):
        part_ref[block] = part[j * half : (j + 1) * half, :]


def input_part(k, hidden_grad, pieces, gate_weight, up_weight, grads):
    blocks, rows, units = hidden_grad.shape
    half = jax.ShapeDtypeStruct((blocks, rows // 2, gate_weight.shape[1]), F32)
    grad = jax.ShapeDtypeStruct((2, blocks, rows // 2, units), BF16)
    return pl.pallas_call(
        functools.partial(input_kernel, k),
        out_shape=(half, grad, grad),
        in_specs=[VMEM] * (7 + len(grads)),
        out_specs=(VMEM,) * 3,
        compiler_params=params(12),
    )(*pieces, hidden_grad, gate_weight, up_weight, *grads)


def body(layer_input, out_grad, gate_pre, up_pre, gate_weight, up_weight, down_weight):
    copies, pre = front(out_grad, layer_input, gate_pre, up_pre)
    far = lax.all_to_all(copies, ("gy", "gz"), 0, 0, axis_index_groups=FAR_PLACES)
    pre_pair = same_pair(pre)
    near, four, near_in, four_in = pack(far, pre_pair)
    pieces = along_x(pre_pair)
    mine = merge(four, near_places(near, four), pieces[1:])
    grad_cols, part = hidden_part(mine, swap_core(mine), down_weight, [])
    parts = lax.all_to_all(part, "gx", 0, 0)
    mine_in = merge(four_in, near_places(near_in, four_in), [])
    hidden_grad = lax.all_to_all(sum_copies(parts, [mine_in]), "gx", 0, 0)
    weights = (gate_weight.T, up_weight.T)
    send, gate_grad, up_grad = input_part(1, hidden_grad, pieces, *weights, [])
    keep, gate_grad, up_grad = input_part(
        0, hidden_grad, pieces, *weights, [gate_grad, up_grad]
    )
    total = (keep + swap_core(send)).astype(BF16).reshape(16, ROWS, -1)
    totals = lax.all_to_all(total, ("gy", "gz"), 0, 0, axis_index_groups=SAME_CORE)
    input_sum = last_sum(totals)
    hidden = hidden_rows(pieces)
    gate_grad, up_grad, hidden = (v.reshape(512, -1) for v in (gate_grad, up_grad, hidden))
    input_cols = place_rows(mine_in, swap_core(mine_in))
    gate_sum = lax.dot_general(input_cols, gate_grad, BY_TOKEN, preferred_element_type=F32)
    up_sum = lax.dot_general(input_cols, up_grad, BY_TOKEN, preferred_element_type=F32)
    down_sum = lax.dot_general(hidden, grad_cols, BY_TOKEN, preferred_element_type=F32)
    return (
        input_sum,
        gate_sum.astype(BF16),
        up_sum.astype(BF16),
        down_sum.astype(BF16),
    )


def solution(mesh):
    tokens = P(("gy", "gz"), "gx")
    hidden = P("gx", ("gy", "gz"))
    return jax.shard_map(
        body,
        mesh=mesh,
        in_specs=(tokens, tokens, hidden, hidden, hidden, hidden, tokens),
        out_specs=(tokens, hidden, hidden, tokens),
        check_vma=False,
    )
```

```python
import functools

import jax
import jax.numpy as jnp
from jax import lax
from jax.experimental import pallas as pl
from jax.experimental.pallas import tpu as pltpu
from jax.sharding import PartitionSpec as P

F32 = jnp.float32
BF16 = jnp.bfloat16
BY_FEATURE = (((1,), (1,)), ((), ()))
BY_TOKEN = (((0,), (0,)), ((), ()))
ROWS = 16
NZ = 8

OWN = ((0, 0), (0, 1), (4, 0), (4, 1))
PREV = ((-1, 0), (-1, 1), (3, 0), (3, 1))
NEXT = ((1, 0), (1, 1), (5, 0), (5, 1))
PREV2 = ((-2, 0), (-2, 1))
NEXT2 = ((2, 0), (2, 1))
ORDER = OWN + PREV + NEXT + PREV2 + NEXT2


def gy_shift(step):
    return [(i, (i + step) % NZ) for i in range(NZ)]


OTHER_CORE = [(i, i ^ 1) for i in range(4)]
FAR_PLACES = [
    [(z + 4 * a) * 4 + 2 * y + core for a in range(2) for y in range(2)]
    for z in range(4)
    for core in range(2)
]
SAME_CORE = [[2 * k + core for k in range(16)] for core in range(2)]

ANY = pl.BlockSpec(memory_space=pl.ANY)
VMEM = pl.BlockSpec(memory_space=pltpu.VMEM)


def params(mib):
    return pltpu.CompilerParams(vmem_limit_bytes=mib * 2**20)


def row_of(there, second):
    z, y = lax.axis_index("gy"), lax.axis_index("gz") // 2
    step, flip = there
    block = second * 2 * NZ + lax.rem(z + step + NZ, NZ) * 2 + (y + flip - 2 * y * flip)
    return pl.multiple_of(block * ROWS, ROWS)


def near_places(near, four):
    return (
        lax.ppermute(near, "gy", gy_shift(2)),
        lax.ppermute(near, "gy", gy_shift(-2)),
        lax.ppermute(four, "gy", gy_shift(1)),
        lax.ppermute(four, "gy", gy_shift(-1)),
    )


def swap_core(x):
    return lax.ppermute(x, "gz", OTHER_CORE)


def front_kernel(*refs):
    ins, (far_ref, pre_ref, tokens, held, sems) = refs[:4], refs[4:]
    parts = (tokens.at[pl.ds(0, ROWS)], tokens.at[pl.ds(ROWS, ROWS)], held.at[0], held.at[1])
    loads = [
        pltpu.make_async_copy(src, dst, sems.at[k]) for k, (src, dst) in enumerate(zip(ins, parts))
    ]
    for load in loads:
        load.start()
    for load in loads:
        load.wait()
    core = lax.axis_index("gz") % 2
    for k in range(2):
        blocks = [held[k, j * ROWS : (j + 1) * ROWS, :] for j in range(4)]
        for y in range(2):
            for second in range(2):
                pre_ref[pl.ds((4 * k + 2 * second + y) * ROWS, ROWS), :] = jnp.where(
                    core == 0, blocks[2 * y + second], blocks[2 * y + 1 - second]
                )
    for k in range(far_ref.shape[0]):
        far_ref[k] = tokens[...]


def front(x, y, gate, up):
    rows, units = gate.shape
    return pl.pallas_call(
        front_kernel,
        out_shape=(
            jax.ShapeDtypeStruct((4, 2 * ROWS, x.shape[1]), BF16),
            jax.ShapeDtypeStruct((2 * rows, units), BF16),
        ),
        in_specs=[ANY] * 4,
        out_specs=(VMEM, VMEM),
        scratch_shapes=[
            pltpu.VMEM((2 * ROWS, x.shape[1]), BF16),
            pltpu.VMEM((2, rows, units), BF16),
            pltpu.SemaphoreType.DMA((4,)),
        ],
        compiler_params=params(58),
    )(x, y, gate, up)


def pack_kernel(far_ref, _, *outs):
    a, y = lax.axis_index("gy") // 4, lax.axis_index("gz") // 2
    for k, (far, flip) in enumerate(((0, 0), (0, 1), (1, 0), (1, 1))):
        there = (a + far - 2 * a * far) * 2 + (y + flip - 2 * y * flip)
        rows = pl.ds(k * ROWS, ROWS)
        for j in range(2):
            near_ref, four_ref = outs[2 * j : 2 * j + 2]
            block = far_ref[there, j * ROWS : (j + 1) * ROWS, :]
            four_ref[rows, :] = block
            if k < 2:
                near_ref[rows, :] = block


def pack(far, earlier):
    _, rows, cols = far.shape
    near = jax.ShapeDtypeStruct((rows, cols), far.dtype)
    four = jax.ShapeDtypeStruct((2 * rows, cols), far.dtype)
    return pl.pallas_call(
        pack_kernel,
        out_shape=(near, four, near, four),
        in_specs=[VMEM, ANY],
        out_specs=(VMEM,) * 4,
        compiler_params=params(4),
    )(far, earlier)


def merge_kernel(four_ref, prev_ref, next_ref, prev2_ref, next2_ref, *refs):
    out_ref = refs[-1]
    k = 0
    for ref in (four_ref, prev_ref, next_ref, prev2_ref, next2_ref):
        out_ref[pl.ds(k, ref.shape[0]), :] = ref[...]
        k += ref.shape[0]


def merge(four, got, earlier):
    prev2, next2, prev, following = got
    return pl.pallas_call(
        merge_kernel,
        out_shape=jax.ShapeDtypeStruct((16 * ROWS, four.shape[1]), four.dtype),
        in_specs=[VMEM] * 5 + [ANY] * len(earlier),
        out_specs=VMEM,
        compiler_params=params(4),
    )(four, prev, following, prev2, next2, *earlier)


def place_kernel(mine_ref, other_ref, out_ref):
    for k, there in enumerate(ORDER):
        rows = pl.ds(k * ROWS, ROWS)
        out_ref[pl.ds(row_of(there, 0), ROWS), :] = mine_ref[rows, :]
        out_ref[pl.ds(row_of(there, 1), ROWS), :] = other_ref[rows, :]


def place_rows(mine, other):
    rows, cols = mine.shape
    return pl.pallas_call(
        place_kernel,
        out_shape=jax.ShapeDtypeStruct((2 * rows, cols), mine.dtype),
        in_specs=[VMEM] * 2,
        out_specs=VMEM,
        compiler_params=params(8),
    )(mine, other)


def hidden_kernel(mine_ref, other_ref, weight_ref, *refs):
    cols_ref, out_ref = refs[-2:]
    place_kernel(mine_ref, other_ref, cols_ref)
    blocks, rows, units = out_ref.shape
    half = blocks * rows // 2
    for k in range(2):
        part = lax.dot_general(
            cols_ref[pl.ds(k * half, half), :],
            weight_ref[...],
            BY_FEATURE,
            preferred_element_type=F32,
        )
        out_ref[:, pl.ds(k * rows // 2, rows // 2), :] = part.astype(BF16).reshape(
            blocks, rows // 2, units
        )


def hidden_part(mine, other, weight, earlier):
    rows, cols = mine.shape
    return pl.pallas_call(
        hidden_kernel,
        out_shape=(
            jax.ShapeDtypeStruct((2 * rows, cols), BF16),
            jax.ShapeDtypeStruct((8, rows // 4, weight.shape[0]), BF16),
        ),
        in_specs=[VMEM] * 3 + [ANY] * len(earlier),
        out_specs=(VMEM, VMEM),
        compiler_params=params(16),
    )(mine, other, weight, *earlier)


def sum_kernel(parts_ref, *refs):
    out_ref = refs[-1]
    total = parts_ref[0].astype(F32)
    for k in range(1, parts_ref.shape[0]):
        total = total + parts_ref[k].astype(F32)
    total = total.astype(BF16)
    for k in range(out_ref.shape[0]):
        out_ref[k] = total


def sum_copies(parts, earlier):
    return pl.pallas_call(
        sum_kernel,
        out_shape=jax.ShapeDtypeStruct(parts.shape, BF16),
        in_specs=[VMEM] + [ANY] * len(earlier),
        out_specs=VMEM,
        compiler_params=params(8),
    )(parts, *earlier)


def stack_kernel(x_ref, y_ref, out_ref):
    rows = x_ref.shape[0]
    out_ref[:rows, :] = x_ref[...]
    out_ref[rows:, :] = y_ref[...]


def stack(x, y):
    rows, cols = x.shape
    return pl.pallas_call(
        stack_kernel,
        out_shape=jax.ShapeDtypeStruct((2 * rows, cols), x.dtype),
        in_specs=[VMEM] * 2,
        out_specs=VMEM,
        compiler_params=params(4),
    )(x, y)


STEPS = (0, 2, 6, 4)


def blocks_of(pieces):
    me = lax.axis_index("gx")
    rows = pieces[0].shape[0] // 4
    for step, ref in zip(STEPS, pieces):
        block = lax.rem(me + 8 - step, 8)
        for k in range(2):
            yield block + k * (1 - 2 * lax.rem(block, 2)), ref, 2 * k * rows, rows


def hidden_rows_kernel(*refs):
    pieces, out_ref = refs[:4], refs[-1]
    for block, ref, first, rows in blocks_of(pieces):
        gate = ref[first : first + rows, :].astype(F32)
        up_value = ref[first + rows : first + 2 * rows, :].astype(F32)
        hidden = (gate * jax.nn.sigmoid(gate) * up_value).astype(BF16)
        for k in range(2):
            out_ref[k, block] = hidden[k * rows // 2 : (k + 1) * rows // 2, :]


def hidden_rows(pieces):
    rows, units = pieces[0].shape
    return pl.pallas_call(
        hidden_rows_kernel,
        out_shape=jax.ShapeDtypeStruct((2, 8, rows // 8, units), BF16),
        in_specs=[VMEM] * 4,
        out_specs=VMEM,
        compiler_params=params(12),
    )(*pieces)


def same_pair(x):
    return stack(x, lax.ppermute(x, "gx", [(i, i ^ 1) for i in range(8)]))


def along_x(pair):
    return [pair] + [
        lax.ppermute(pair, "gx", [(i, (i + step) % 8) for i in range(8)]) for step in (2, 6, 4)
    ]


def last_sum_kernel(parts_ref, out_ref):
    total = parts_ref[0].astype(F32)
    for k in range(1, parts_ref.shape[0]):
        total = total + parts_ref[k].astype(F32)
    out_ref[...] = total.astype(BF16)


def last_sum(parts):
    return pl.pallas_call(
        last_sum_kernel,
        out_shape=jax.ShapeDtypeStruct(parts.shape[1:], BF16),
        in_specs=[VMEM],
        out_specs=VMEM,
        compiler_params=params(4),
    )(parts)


def input_kernel(k, *refs):
    pieces, (hid_ref, gw_ref, uw_ref), refs = refs[:4], refs[4:7], refs[7:]
    part_ref, gg_ref, ug_ref = refs[-3:]
    half = hid_ref.shape[1] // 2
    gate_grads, up_grads, places = [], [], []
    for block, piece, first, rows in blocks_of(pieces):
        hidden_grad = hid_ref[block, k * half : (k + 1) * half, :].astype(F32)
        gate = piece[first + k * half : first + (k + 1) * half, :].astype(F32)
        first = first + rows
        up_value = piece[first + k * half : first + (k + 1) * half, :].astype(F32)
        sigmoid_gate = jax.nn.sigmoid(gate)
        gate_grad = hidden_grad * up_value * sigmoid_gate * (1.0 + gate * (1.0 - sigmoid_gate))
        gate_grads.append(gate_grad.astype(BF16))
        up_grads.append((hidden_grad * (gate * sigmoid_gate)).astype(BF16))
        places.append(block)
        gg_ref[k, block] = gate_grads[-1]
        ug_ref[k, block] = up_grads[-1]
    if len(refs) > 3:
        gg_ref[1 - k] = refs[0][1 - k]
        ug_ref[1 - k] = refs[1][1 - k]
    part = jnp.dot(
        jnp.concatenate(gate_grads, axis=0), gw_ref[...], preferred_element_type=F32
    ) + jnp.dot(jnp.concatenate(up_grads, axis=0), uw_ref[...], preferred_element_type=F32)
    for j, block in enumerate(places):
        part_ref[block] = part[j * half : (j + 1) * half, :].astype(part_ref.dtype)


def input_part(k, hidden_grad, pieces, gate_weight, up_weight, grads):
    blocks, rows, units = hidden_grad.shape
    half = jax.ShapeDtypeStruct((blocks, rows // 2, gate_weight.shape[1]), BF16 if k else F32)
    grad = jax.ShapeDtypeStruct((2, blocks, rows // 2, units), BF16)
    return pl.pallas_call(
        functools.partial(input_kernel, k),
        out_shape=(half, grad, grad),
        in_specs=[VMEM] * (7 + len(grads)),
        out_specs=(VMEM,) * 3,
        compiler_params=params(12),
    )(*pieces, hidden_grad, gate_weight, up_weight, *grads)


def body(layer_input, out_grad, gate_pre, up_pre, gate_weight, up_weight, down_weight):
    copies, pre = front(out_grad, layer_input, gate_pre, up_pre)
    far = lax.all_to_all(copies, ("gy", "gz"), 0, 0, axis_index_groups=FAR_PLACES)
    pre_pair = same_pair(pre)
    near, four, near_in, four_in = pack(far, pre_pair)
    pieces = along_x(pre_pair)
    mine = merge(four, near_places(near, four), pieces[1:])
    grad_cols, part = hidden_part(mine, swap_core(mine), down_weight, [])
    parts = lax.all_to_all(part, "gx", 0, 0)
    mine_in = merge(four_in, near_places(near_in, four_in), [])
    hidden_grad = lax.all_to_all(sum_copies(parts, [mine_in]), "gx", 0, 0)
    weights = (gate_weight.T, up_weight.T)
    send, gate_grad, up_grad = input_part(1, hidden_grad, pieces, *weights, [])
    keep, gate_grad, up_grad = input_part(
        0, hidden_grad, pieces, *weights, [gate_grad, up_grad]
    )
    total = (keep + swap_core(send).astype(F32)).astype(BF16).reshape(16, ROWS, -1)
    totals = lax.all_to_all(total, ("gy", "gz"), 0, 0, axis_index_groups=SAME_CORE)
    input_sum = last_sum(totals)
    hidden = hidden_rows(pieces)
    gate_grad, up_grad, hidden = (v.reshape(512, -1) for v in (gate_grad, up_grad, hidden))
    input_cols = place_rows(mine_in, swap_core(mine_in))
    gate_sum = lax.dot_general(input_cols, gate_grad, BY_TOKEN, preferred_element_type=F32)
    up_sum = lax.dot_general(input_cols, up_grad, BY_TOKEN, preferred_element_type=F32)
    down_sum = lax.dot_general(hidden, grad_cols, BY_TOKEN, preferred_element_type=F32)
    return (
        input_sum,
        gate_sum.astype(BF16),
        up_sum.astype(BF16),
        down_sum.astype(BF16),
    )


def solution(mesh):
    tokens = P(("gy", "gz"), "gx")
    hidden = P("gx", ("gy", "gz"))
    return jax.shard_map(
        body,
        mesh=mesh,
        in_specs=(tokens, tokens, hidden, hidden, hidden, hidden, tokens),
        out_specs=(tokens, hidden, hidden, tokens),
        check_vma=False,
    )
```
